32 devices in a mesh: groups: 2 (over y), scan: 4 (over z), depth: 4 (over x, core).
Axes of the slice: x: 2, y: 2, z: 4, core: 2. Of those that a mesh axis runs over, the one named last changes fastest.
Arguments:
- probe: float32 [2, 256, 256], replicated, may hold values from -6 to 6
- slices: float32 [8, 2, 2048, 1024], P('depth', None, ('groups', 'scan')), parts along dimension 2, may hold values from -3 to 3, as said below
- positions: int32 [16, 2], P(('groups', 'scan')), parts along dimension 0, may hold values from 0 to 768, as said below
- counts: int32 [8], P(('groups', 'scan')), parts along dimension 0, may hold values from 1 to 2, as said below
- amplitude: float32 [16, 256, 256], P(('groups', 'scan')), parts along dimension 0, may hold values from 0.2 to 3
Outputs:
- gradient: float32 [8, 2, 2048, 1024], P('depth', None, ('groups', 'scan')), parts along dimension 2
The draws below stay inside these ranges and needn't reach their ends.
There are 2 independent parts, one for each index of `groups`. The reference program is written for one: setup_inputs(seed, part) draws one part's arguments, and reference() takes and returns one part's arrays. A program takes and returns all parts, laid end to end along the dimension named above; an argument that names none is the same for every part. Nothing has to cross between parts.
Inputs may be any that keep to these rules, and one draw needn't show every extreme that they name: `positions`: row offsets lie in 0 to 255 and column offsets in 0 to 768; both ends of both ranges are taken. `counts`: each tile has 1 to 2 live patches, in its first slots; some tile has 2 and some has 1. `slices`: transmission of magnitude between exp(-1) and exp(1).
All inputs are finite; a program needn't handle non-finite values.
Results may differ from the reference program's by a relative error of at most 0.0003.
Values sent between devices are 32-bit elements; how exact they have to be, the bound alone decides.
A program may use at most 128 MiB of HBM per device.

```python
import math
import jax
import jax.numpy as jnp
from jax import lax

PATCH = 256
WIDTH = 1024
SLOTS = 2
SLICES = 8
TILES = 4
ROWS = 1024


def draw_slices(key, part):
    key_level = jax.random.fold_in(key, 11)
    key_phase = jax.random.fold_in(key, 12)
    shape = (SLICES, ROWS, WIDTH)
    level = jnp.clip(0.25 * jax.random.normal(key_level, shape, jnp.float32), -1.0, 1.0)
    phase = jnp.clip(0.6 * jax.random.normal(key_phase, shape, jnp.float32), -2.4, 2.4)
    magnitude = jnp.exp(level)
    return jnp.stack([magnitude * jnp.cos(phase), magnitude * jnp.sin(phase)], axis=1)


def draw_positions(key, part):
    total = ROWS // PATCH * SLOTS
    row_offsets = jax.random.randint(jax.random.fold_in(key, 21), (total,), 0, PATCH)
    col_offsets = jax.random.randint(jax.random.fold_in(key, 22), (total,), 0, WIDTH - PATCH + 1)
    first = jax.random.randint(jax.random.fold_in(key, 23), (), 0, total)
    second = (first + 1) % total
    row_offsets = row_offsets.at[first].set(PATCH - 1).at[second].set(0)
    col_offsets = col_offsets.at[first].set(WIDTH - PATCH).at[second].set(0)
    return jnp.stack([row_offsets, col_offsets], axis=1).astype(jnp.int32)


def draw_counts(key, part):
    tiles = ROWS // PATCH
    values = jax.random.randint(jax.random.fold_in(key, 31), (tiles,), 1, SLOTS + 1)
    first = jax.random.randint(jax.random.fold_in(key, 32), (), 0, tiles)
    second = (first + 1) % tiles
    return values.at[first].set(SLOTS).at[second].set(1).astype(jnp.int32)


def block_scale(stream_key, extent, shards, low, largest):
    level = 1.0
    for position, shards_of in shards:
        heights = jax.random.uniform(jax.random.fold_in(jax.random.fold_in(stream_key, 6), position), (shards_of,), jnp.float32, low / len(shards), largest / len(shards))
        level = level * jnp.repeat(jnp.exp(heights), extent[position] // shards_of).reshape((-1,) + (1,) * (len(extent) - 1 - position))
    return level


def gaussian(key, shape, width, limit, kind=jnp.bfloat16):
    drawn = jax.random.normal(key, shape, jnp.float32) * width
    return jnp.minimum(jnp.maximum(drawn, -limit), limit).astype(kind)


def setup_inputs(seed: int = 0, part: int = 0) -> dict:
    splits = jax.random.split(jax.random.key(seed), 6)
    own_keys = jax.random.split(jax.random.fold_in(splits[5], part), 6)
    probe = gaussian(splits[0], (2, PATCH, PATCH), 1.0, 6.0, jnp.float32)
    slices = draw_slices(jax.random.fold_in(jax.random.fold_in(splits[5], part), 71), part)
    positions = draw_positions(jax.random.fold_in(jax.random.fold_in(splits[5], part), 71), part)
    counts = draw_counts(jax.random.fold_in(jax.random.fold_in(splits[5], part), 71), part)
    amplitude = jnp.clip(jnp.exp(math.log(3.0) - 2.7080502 * jax.random.uniform(own_keys[4], (TILES * SLOTS, PATCH, PATCH), jnp.float32) ** block_scale(own_keys[4], (TILES * SLOTS, PATCH, PATCH), ((0, 4),), -0.2, 0.2)), 0.2, 3.0)
    return {"probe": probe, "slices": slices, "positions": positions, "counts": counts, "amplitude": amplitude}


chirp_rate = 0.25

def make_tables(length):
    index = jnp.arange(length, dtype=jnp.int32)
    product = index[:, None] * index[None, :] % length
    angle = 2.0 * math.pi / length * product.astype(jnp.float32)
    factor = 1.0 / math.sqrt(length)
    table_real = (jnp.cos(angle) * factor).astype(jnp.float32)
    table_imag = (-jnp.sin(angle) * factor).astype(jnp.float32)
    freq = jnp.where(index < length // 2, index, index - length).astype(jnp.float32)
    theta = -math.pi * chirp_rate / length * (freq[:, None] ** 2 + freq[None, :] ** 2)
    return (table_real, table_imag, jnp.cos(theta), jnp.sin(theta))

def left_product(matrix, field):
    return jnp.einsum('jk,...kl->...jl', matrix.astype(jnp.float32), field.astype(jnp.float32), precision=lax.Precision.HIGHEST)

def right_product(field, matrix):
    return jnp.einsum('...jk,kl->...jl', field.astype(jnp.float32), matrix.astype(jnp.float32), precision=lax.Precision.HIGHEST)

def transform(field, tables, forward):
    table_real = tables[0]
    table_imag = tables[1] if forward else -tables[1]
    real_part = field[..., 0, :, :]
    imag_part = field[..., 1, :, :]
    first_real = left_product(table_real, real_part) - left_product(table_imag, imag_part)
    first_imag = left_product(table_real, imag_part) + left_product(table_imag, real_part)
    out_real = right_product(first_real, table_real) - right_product(first_imag, table_imag)
    out_imag = right_product(first_real, table_imag) + right_product(first_imag, table_real)
    return jnp.stack([out_real, out_imag], axis=-3)

def complex_product(first, second, conjugate):
    first_real = first[..., 0, :, :].astype(jnp.float32)
    first_imag = first[..., 1, :, :].astype(jnp.float32)
    if conjugate:
        first_imag = -first_imag
    second_real = second[..., 0, :, :].astype(jnp.float32)
    second_imag = second[..., 1, :, :].astype(jnp.float32)
    return jnp.stack([first_real * second_real - first_imag * second_imag, first_real * second_imag + first_imag * second_real], axis=-3)

def propagate(field, tables, forward):
    spectrum = transform(field, tables, True)
    sine = tables[3] if forward else -tables[3]
    chirp = jnp.stack([tables[2], sine], axis=0)
    return transform(complex_product(spectrum, chirp, False), tables, False)

def far_field(exit_wave, measured, live, tables):
    spectrum = transform(exit_wave, tables, True)
    power = spectrum[..., 0, :, :] ** 2 + spectrum[..., 1, :, :] ** 2
    keep = live * (1.0 - measured.astype(jnp.float32) / jnp.sqrt(power + 1.0))
    residual = spectrum * keep[..., None, :, :]
    return transform(residual, tables, False)

def reference(probe, slices, positions, counts, amplitude):
    tables = make_tables(PATCH)
    tiles = ROWS // PATCH
    places = positions.astype(jnp.int32)
    live_counts = counts.astype(jnp.int32)
    extended = jnp.concatenate([slices, slices[:, :, :PATCH]], axis=2).astype(jnp.float32)
    start_wave = probe.astype(jnp.float32)

    def one_patch(grad_ext, index):
        index = index.astype(jnp.int32)
        tile = (index // SLOTS).astype(jnp.int32)
        slot = (index % SLOTS).astype(jnp.int32)
        row = (tile * PATCH + places[index, 0]).astype(jnp.int32)
        column = places[index, 1].astype(jnp.int32)
        zero = jnp.zeros((), jnp.int32)
        window = lax.dynamic_slice(extended, (zero, zero, row, column), (SLICES, 2, PATCH, PATCH))
        live = (slot < live_counts[tile]).astype(jnp.float32)
        wave_now = start_wave
        saved = []
        for layer in range(SLICES):
            psi = propagate(wave_now, tables, True)
            saved.append(psi)
            wave_now = complex_product(psi, window[layer], False)
        chi_wave = far_field(wave_now, amplitude[index], live, tables)
        terms = [None] * SLICES
        for layer in range(SLICES - 1, -1, -1):
            terms[layer] = complex_product(saved[layer], chi_wave, True)
            if layer > 0:
                back = complex_product(window[layer], chi_wave, True)
                chi_wave = propagate(back, tables, False)
        stacked = jnp.stack(terms, axis=0)
        current = lax.dynamic_slice(grad_ext, (zero, zero, row, column), (SLICES, 2, PATCH, PATCH))
        updated = (current + stacked).astype(grad_ext.dtype)
        grad_ext = lax.dynamic_update_slice(grad_ext, updated, (zero, zero, row, column))
        return (grad_ext, None)
    grad_ext = jnp.zeros((SLICES, 2, ROWS + PATCH, WIDTH), jnp.float32)
    grad_ext, _ = lax.scan(one_patch, grad_ext, jnp.arange(tiles * SLOTS, dtype=jnp.int32))
    return grad_ext[:, :, :ROWS].at[:, :, :PATCH].add(grad_ext[:, :, ROWS:])
```

```python
import functools
import math

import jax
import jax.numpy as jnp
import numpy as np
from jax import lax
from jax.experimental import pallas as pl
from jax.experimental.pallas import tpu as pltpu
from jax.sharding import PartitionSpec as P

chirp_rate = 0.25
CHUNK = 32


def make_tables(length):
    index = np.arange(length)
    angle = 2.0 * np.pi / length * (index[:, None] * index[None, :] % length)
    forward = (np.cos(angle) - 1j * np.sin(angle)) / math.sqrt(length)
    freq = np.where(index < length // 2, index, index - length).astype(np.float64)
    chirp = np.exp(-1j * np.pi * chirp_rate / length * freq**2)
    step = (np.conj(forward) * chirp[None, :]) @ forward
    left_hi, left_lo, right_hi, right_lo = [], [], [], []
    for table in (step, forward):
        real, imag = table.real, table.imag
        left = np.block([[real, -imag], [imag, real]]).astype(np.float32)
        right = np.block([[real, imag], [-imag, real]]).astype(np.float32)
        for whole, highs, lows in ((left, left_hi, left_lo), (right, right_hi, right_lo)):
            high = whole.astype(jnp.bfloat16)
            highs.append(high)
            lows.append((whole - high.astype(np.float32)).astype(jnp.bfloat16))
    return tuple(np.stack(parts) for parts in (left_hi, left_lo, right_hi, right_lo))


def dot(a, b):
    return jnp.dot(a, b, preferred_element_type=jnp.float32)


def split(x):
    high = x.astype(jnp.bfloat16)
    low = (x - high.astype(jnp.float32)).astype(jnp.bfloat16)
    return high, low


def kernel(
    tiles, groups,
    probe, slices, pos, amp, live, left_hi, left_lo, right_hi, right_lo,
    out,
    pieces, win, nbr, psi, wave_in, wave_out, chi_in, chi_out, terms, terms_in, pos_in, cur,
    pos_sem, piece_send, piece_recv, wave_send, wave_recv, chi_send, chi_recv, term_send, term_recv,
):
    slots, layers, _, size, _ = pieces.shape
    blocks = slices.shape[-1] // size
    tile = lax.axis_index("scan")
    group = lax.axis_index("depth")
    last = groups - 1
    next_tile = lax.rem(tile + 1, tiles)
    prev_tile = lax.rem(tile + tiles - 1, tiles)
    next_group = lax.rem(group + 1, groups)
    prev_group = lax.rem(group + groups - 1, groups)

    def remote(src, dst, send, recv, where):
        return pltpu.make_async_remote_copy(
            src_ref=src, dst_ref=dst, send_sem=send, recv_sem=recv,
            device_id=where, device_id_type=pl.DeviceIdType.MESH,
        )

    def piece_copy(s, l):
        return remote(pieces.at[s, l], nbr.at[s, l], piece_send.at[s, l], piece_recv.at[s, l], {"scan": prev_tile})

    def term_copy(s, l):
        return remote(terms.at[s, l], terms_in.at[s, l], term_send.at[s, l], term_recv.at[s, l], {"scan": next_tile})

    def wave_copy(s):
        return remote(wave_out.at[s], wave_in.at[s], wave_send.at[s], wave_recv.at[s], {"depth": next_group})

    def chi_copy(s):
        return remote(chi_out.at[s], chi_in.at[s], chi_send.at[s], chi_recv.at[s], {"depth": prev_group})

    barrier = pltpu.get_barrier_semaphore()
    for where in ({"scan": next_tile}, {"scan": prev_tile}, {"depth": next_group}, {"depth": prev_group}):
        pl.semaphore_signal(barrier, inc=1, device_id=where, device_id_type=pl.DeviceIdType.MESH)
    pl.semaphore_wait(barrier, 4)

    pos_copy = remote(pos, pos_in, pos_sem.at[0], pos_sem.at[1], {"scan": next_tile})
    pos_copy.start()

    def rows_of(chunk):
        return pl.ds(pl.multiple_of(chunk * CHUNK, CHUNK), CHUNK)

    def iotas(chunk):
        row = lax.broadcasted_iota(jnp.int32, (CHUNK, size), 0) + chunk * CHUNK
        column = lax.broadcasted_iota(jnp.int32, (CHUNK, size), 1)
        return row, column

    def inside(column, block, start):
        offset = column + block * size - start
        return (offset >= 0) & (offset < size)

    def cut(places, target, s, l, own):
        def one(chunk, carry):
            row, column = iotas(chunk)
            keep = row >= places[s, 0, 0:1, :]
            if not own:
                keep = jnp.logical_not(keep)
            start = places[s, 1, 0:1, :]
            for part in range(2):
                value = jnp.zeros((CHUNK, size), jnp.float32)
                for block in range(blocks):
                    value = jnp.where(
                        inside(column, block, start),
                        slices[l, part, rows_of(chunk), block * size : (block + 1) * size],
                        value,
                    )
                target[s, l, part, rows_of(chunk), :] = jnp.where(keep, value, 0.0)
            return carry

        lax.fori_loop(0, size // CHUNK, one, 0)

    def add_terms(places, source, s, l, own):
        def one(chunk, carry):
            row, column = iotas(chunk)
            keep = row >= places[s, 0, 0:1, :]
            if not own:
                keep = jnp.logical_not(keep)
            start = places[s, 1, 0:1, :]
            for part in range(2):
                value = jnp.where(keep, source[s, l, part, rows_of(chunk), :], 0.0)
                for block in range(blocks):
                    out[l, part, rows_of(chunk), block * size : (block + 1) * size] += jnp.where(
                        inside(column, block, start), value, 0.0
                    )
            return carry

        lax.fori_loop(0, size // CHUNK, one, 0)

    def two_sided(which, real, imag):
        high, low = split(jnp.concatenate([real, imag], axis=1))
        y = dot(high, right_hi[which]) + dot(high, right_lo[which]) + dot(low, right_hi[which])
        high, low = split(jnp.concatenate([y[:, :size], y[:, size:]], axis=0))
        z = dot(left_hi[which], high) + dot(left_lo[which], high) + dot(left_hi[which], low)
        return z[:size], z[size:]

    pos_copy.wait_recv()

    for s in range(slots):
        for l in range(layers):
            cut(pos_in, pieces, s, l, False)
            piece_copy(s, l).start()

    out[...] = jnp.zeros_like(out)
    for s in range(slots):
        for l in range(layers):
            cut(pos, win, s, l, True)

    def roll_probe(s):
        row = lax.broadcasted_iota(jnp.int32, (size, size), 0)
        column = lax.broadcasted_iota(jnp.int32, (size, size), 1)
        down = row - column - pos[s, 0, 0:1, :]
        across = column - row - pos[s, 1, 0:1, :]
        rows_shift = jnp.zeros((size, size), jnp.float32)
        for turn in range(2):
            rows_shift = jnp.where(down == -turn * size, 1.0, rows_shift)
        columns_shift = jnp.zeros((size, size), jnp.float32)
        for turn in range(blocks + 1):
            columns_shift = jnp.where(across == -turn * size, 1.0, columns_shift)
        rows_shift = rows_shift.astype(jnp.bfloat16)
        columns_shift = columns_shift.astype(jnp.bfloat16)

        def three(x):
            first = x.astype(jnp.bfloat16)
            rest = x - first.astype(jnp.float32)
            second = rest.astype(jnp.bfloat16)
            third = (rest - second.astype(jnp.float32)).astype(jnp.bfloat16)
            return first, second, third

        for part in range(2):
            a, b, c = three(probe[part])
            x = dot(rows_shift, a) + dot(rows_shift, b) + dot(rows_shift, c)
            a, b, c = three(x)
            wave_in[s, part] = dot(a, columns_shift) + dot(b, columns_shift) + dot(c, columns_shift)

    def forward(s):
        @pl.when(group == 0)
        def _():
            roll_probe(s)

        @pl.when(group > 0)
        def _():
            wave_copy(s).wait_recv()

        for l in range(layers):
            source = wave_in.at[s] if l == 0 else cur
            real, imag = two_sided(0, source[0], source[1])
            psi[s, l, 0] = real
            psi[s, l, 1] = imag
            piece_copy(s, l).wait_recv()
            real, imag = psi[s, l, 0], psi[s, l, 1]
            w_real = win[s, l, 0] + nbr[s, l, 0]
            w_imag = win[s, l, 1] + nbr[s, l, 1]
            target = cur if l < layers - 1 else wave_out.at[s]
            target[0] = real * w_real - imag * w_imag
            target[1] = real * w_imag + imag * w_real

        @pl.when(group < last)
        def _():
            wave_copy(s).start()

        @pl.when(group == last)
        def _():
            real, imag = two_sided(1, wave_out[s, 0], wave_out[s, 1])
            keep = live[s, 0:1, :] * (1.0 - amp[s] / jnp.sqrt(real * real + imag * imag + 1.0))
            cur[0] = real * keep
            cur[1] = -(imag * keep)
            real, imag = two_sided(1, cur[0], cur[1])
            chi_in[s, 0] = real
            chi_in[s, 1] = imag

    def adjoint(s):
        @pl.when(group < last)
        def _():
            chi_copy(s).wait_recv()

        for l in range(layers - 1, -1, -1):
            source = chi_in.at[s] if l == layers - 1 else cur
            c_real, c_imag = source[0], source[1]
            terms[s, l, 0] = psi[s, l, 0] * c_real - psi[s, l, 1] * c_imag
            terms[s, l, 1] = -(psi[s, l, 0] * c_imag + psi[s, l, 1] * c_real)
            term_copy(s, l).start()

            def back():
                w_real = win[s, l, 0] + nbr[s, l, 0]
                w_imag = win[s, l, 1] + nbr[s, l, 1]
                c_real, c_imag = source[0], source[1]
                return two_sided(0, w_real * c_real - w_imag * c_imag, w_real * c_imag + w_imag * c_real)

            if l > 0:
                real, imag = back()
                cur[0] = real
                cur[1] = imag
            else:

                @pl.when(group > 0)
                def _():
                    real, imag = back()
                    chi_out[s, 0] = real
                    chi_out[s, 1] = imag
                    chi_copy(s).start()

        for l in range(layers):
            add_terms(pos, terms, s, l, True)

    def task(k, carry):
        at_last = group == last
        is_forward = jnp.where(at_last, lax.rem(k, 2) == 0, k < slots)
        s = jnp.where(at_last, k // 2, lax.rem(k, slots))

        @pl.when(is_forward)
        def _():
            forward(s)

        @pl.when(jnp.logical_not(is_forward))
        def _():
            adjoint(s)

        return carry

    lax.fori_loop(0, 2 * slots, task, 0)

    for s in range(slots):
        for l in range(layers - 1, -1, -1):
            term_copy(s, l).wait_recv()
            add_terms(pos_in, terms_in, s, l, False)

    pos_copy.wait_send()
    for s in range(slots):
        for l in range(layers):
            piece_copy(s, l).wait_send()
            term_copy(s, l).wait_send()

    @pl.when(group < last)
    def _():
        for s in range(slots):
            wave_copy(s).wait_send()

    @pl.when(group > 0)
    def _():
        for s in range(slots):
            chi_copy(s).wait_send()


def solution(mesh):
    tiles, groups = mesh.shape["scan"], mesh.shape["depth"]

    def body(probe, slices, positions, counts, amplitude):
        size = probe.shape[-1]
        slots = positions.shape[0]
        layers = slices.shape[0]
        places = jnp.broadcast_to(positions[:, :, None, None], (slots, 2, 8, size))
        live = (jnp.arange(slots, dtype=jnp.int32) < counts[0]).astype(jnp.float32)
        live = jnp.broadcast_to(live[:, None, None], (slots, 8, size))
        tables = [jnp.asarray(table) for table in make_tables(size)]
        planes = pltpu.VMEM((slots, layers, 2, size, size), jnp.float32)
        waves = pltpu.VMEM((slots, 2, size, size), jnp.float32)
        each = pltpu.SemaphoreType.DMA((slots, layers))
        some = pltpu.SemaphoreType.DMA((slots,))
        return pl.pallas_call(
            functools.partial(kernel, tiles, groups),
            out_shape=jax.ShapeDtypeStruct(slices.shape, jnp.float32),
            in_specs=[pl.BlockSpec(memory_space=pltpu.VMEM)] * 9,
            out_specs=pl.BlockSpec(memory_space=pltpu.VMEM),
            scratch_shapes=[
                planes, planes, planes, planes,
                waves, waves, waves, waves,
                planes, planes,
                pltpu.VMEM((slots, 2, 8, size), jnp.int32),
                pltpu.VMEM((2, size, size), jnp.float32),
                pltpu.SemaphoreType.DMA((2,)),
                each, each, some, some, some, some, each, each,
            ],
            compiler_params=pltpu.CompilerParams(
                collective_id=0, has_side_effects=True, vmem_limit_bytes=52 * 1024 * 1024
            ),
        )(probe, slices, places, amplitude, live, *tables)

    return jax.shard_map(
        body,
        mesh=mesh,
        in_specs=(
            P(),
            P("depth", None, ("groups", "scan"), None),
            P(("groups", "scan"), None),
            P(("groups", "scan")),
            P(("groups", "scan"), None, None),
        ),
        out_specs=P("depth", None, ("groups", "scan"), None),
        check_vma=False,
    )
```

```python
import functools
import math

import jax
import jax.numpy as jnp
import numpy as np
from jax import lax
from jax.experimental import pallas as pl
from jax.experimental.pallas import tpu as pltpu
from jax.sharding import PartitionSpec as P

chirp_rate = 0.25
CHUNK = 32


def make_tables(length):
    index = np.arange(length)
    angle = 2.0 * np.pi / length * (index[:, None] * index[None, :] % length)
    forward = (np.cos(angle) - 1j * np.sin(angle)) / math.sqrt(length)
    freq = np.where(index < length // 2, index, index - length).astype(np.float64)
    chirp = np.exp(-1j * np.pi * chirp_rate / length * freq**2)
    step = (np.conj(forward) * chirp[None, :]) @ forward
    left_hi, left_lo, right_hi, right_lo = [], [], [], []
    for table in (step, forward):
        real, imag = table.real, table.imag
        left = np.block([[real, -imag], [imag, real]]).astype(np.float32)
        right = np.block([[real, imag], [-imag, real]]).astype(np.float32)
        for whole, highs, lows in ((left, left_hi, left_lo), (right, right_hi, right_lo)):
            high = whole.astype(jnp.bfloat16)
            highs.append(high)
            lows.append((whole - high.astype(np.float32)).astype(jnp.bfloat16))
    return tuple(np.stack(parts) for parts in (left_hi, left_lo, right_hi, right_lo))


def dot(a, b):
    return jnp.dot(a, b, preferred_element_type=jnp.float32)


def split(x):
    high = x.astype(jnp.bfloat16)
    low = (x - high.astype(jnp.float32)).astype(jnp.bfloat16)
    return high, low


def kernel(
    tiles, groups,
    probe, slices, pos, amp, live, left_hi, left_lo, right_hi, right_lo,
    out,
    pieces, win, nbr, psi, wave_in, wave_out, chi_in, chi_out, terms, terms_in, pos_in, cur,
    pos_sem, piece_send, piece_recv, wave_send, wave_recv, chi_send, chi_recv, term_send, term_recv,
):
    slots, layers, _, size, _ = pieces.shape
    blocks = slices.shape[-1] // size
    tile = lax.axis_index("scan")
    group = lax.axis_index("depth")
    last = groups - 1
    next_tile = lax.rem(tile + 1, tiles)
    prev_tile = lax.rem(tile + tiles - 1, tiles)
    next_group = lax.rem(group + 1, groups)
    prev_group = lax.rem(group + groups - 1, groups)

    def remote(src, dst, send, recv, where):
        return pltpu.make_async_remote_copy(
            src_ref=src, dst_ref=dst, send_sem=send, recv_sem=recv,
            device_id=where, device_id_type=pl.DeviceIdType.MESH,
        )

    def piece_copy(s, l):
        return remote(pieces.at[s, l], nbr.at[s, l], piece_send.at[s, l], piece_recv.at[s, l], {"scan": prev_tile})

    def term_copy(s, l):
        return remote(terms.at[s, l], terms_in.at[s, l], term_send.at[s, l], term_recv.at[s, l], {"scan": next_tile})

    def wave_copy(s):
        return remote(wave_out.at[s], wave_in.at[s], wave_send.at[s], wave_recv.at[s], {"depth": next_group})

    def chi_copy(s):
        return remote(chi_out.at[s], chi_in.at[s], chi_send.at[s], chi_recv.at[s], {"depth": prev_group})

    barrier = pltpu.get_barrier_semaphore()
    for where in ({"scan": next_tile}, {"scan": prev_tile}, {"depth": next_group}, {"depth": prev_group}):
        pl.semaphore_signal(barrier, inc=1, device_id=where, device_id_type=pl.DeviceIdType.MESH)
    pl.semaphore_wait(barrier, 4)

    pos_copy = remote(pos, pos_in, pos_sem.at[0], pos_sem.at[1], {"scan": next_tile})
    pos_copy.start()

    def rows_of(chunk):
        return pl.ds(pl.multiple_of(chunk * CHUNK, CHUNK), CHUNK)

    def iotas(chunk):
        row = lax.broadcasted_iota(jnp.int32, (CHUNK, size), 0) + chunk * CHUNK
        column = lax.broadcasted_iota(jnp.int32, (CHUNK, size), 1)
        return row, column

    def inside(column, block, start):
        offset = column + block * size - start
        return (offset >= 0) & (offset < size)

    def cut(places, target, s, l, own):
        def one(chunk, carry):
            row, column = iotas(chunk)
            keep = row >= places[s, 0, 0:1, :]
            if not own:
                keep = jnp.logical_not(keep)
            start = places[s, 1, 0:1, :]
            for part in range(2):
                value = jnp.zeros((CHUNK, size), jnp.float32)
                for block in range(blocks):
                    value = jnp.where(
                        inside(column, block, start),
                        slices[l, part, rows_of(chunk), block * size : (block + 1) * size],
                        value,
                    )
                target[s, l, part, rows_of(chunk), :] = jnp.where(keep, value, 0.0)
            return carry

        lax.fori_loop(0, size // CHUNK, one, 0)

    def add_terms(places, source, s, l, own):
        def one(chunk, carry):
            row, column = iotas(chunk)
            keep = row >= places[s, 0, 0:1, :]
            if not own:
                keep = jnp.logical_not(keep)
            start = places[s, 1, 0:1, :]
            for part in range(2):
                value = jnp.where(keep, source[s, l, part, rows_of(chunk), :], 0.0)
                for block in range(blocks):
                    out[l, part, rows_of(chunk), block * size : (block + 1) * size] += jnp.where(
                        inside(column, block, start), value, 0.0
                    )
            return carry

        lax.fori_loop(0, size // CHUNK, one, 0)

    def two_sided(which, real, imag):
        high, low = split(jnp.concatenate([real, imag], axis=1))
        y = dot(high, right_hi[which]) + dot(high, right_lo[which]) + dot(low, right_hi[which])
        high, low = split(jnp.concatenate([y[:, :size], y[:, size:]], axis=0))
        z = dot(left_hi[which], high) + dot(left_lo[which], high) + dot(left_hi[which], low)
        return z[:size], z[size:]

    pos_copy.wait_recv()

    for s in range(slots):
        for l in range(layers):
            cut(pos_in, pieces, s, l, False)
            if s == 0:
                piece_copy(s, l).start()

    out[...] = jnp.zeros_like(out)
    for s in range(slots):
        for l in range(layers):
            cut(pos, win, s, l, True)

    def roll_probe(s):
        row = lax.broadcasted_iota(jnp.int32, (size, size), 0)
        column = lax.broadcasted_iota(jnp.int32, (size, size), 1)
        down = row - column - pos[s, 0, 0:1, :]
        across = column - row - pos[s, 1, 0:1, :]
        rows_shift = jnp.zeros((size, size), jnp.float32)
        for turn in range(2):
            rows_shift = jnp.where(down == -turn * size, 1.0, rows_shift)
        columns_shift = jnp.zeros((size, size), jnp.float32)
        for turn in range(blocks + 1):
            columns_shift = jnp.where(across == -turn * size, 1.0, columns_shift)
        rows_shift = rows_shift.astype(jnp.bfloat16)
        columns_shift = columns_shift.astype(jnp.bfloat16)

        def three(x):
            first = x.astype(jnp.bfloat16)
            rest = x - first.astype(jnp.float32)
            second = rest.astype(jnp.bfloat16)
            third = (rest - second.astype(jnp.float32)).astype(jnp.bfloat16)
            return first, second, third

        for part in range(2):
            a, b, c = three(probe[part])
            x = dot(rows_shift, a) + dot(rows_shift, b) + dot(rows_shift, c)
            a, b, c = three(x)
            wave_in[s, part] = dot(a, columns_shift) + dot(b, columns_shift) + dot(c, columns_shift)

    def first_psi(s, carry):
        roll_probe(s)
        propagate(wave_in.at[s], s, 0)
        return carry

    def propagate(source, s, l):
        real, imag = two_sided(0, source[0], source[1])
        psi[s, l, 0] = real
        psi[s, l, 1] = imag

    @pl.when(group == 0)
    def _():
        lax.fori_loop(0, slots, first_psi, 0)

    for s in range(1, slots):
        for l in range(layers):
            piece_copy(s - 1, l).wait_send()
            piece_copy(s, l).start()

    def forward(s):
        @pl.when(group > 0)
        def _():
            wave_copy(s).wait_recv()
            propagate(wave_in.at[s], s, 0)

        for l in range(layers):
            if l > 0:
                propagate(cur, s, l)
            piece_copy(s, l).wait_recv()
            real, imag = psi[s, l, 0], psi[s, l, 1]
            w_real = win[s, l, 0] + nbr[s, l, 0]
            w_imag = win[s, l, 1] + nbr[s, l, 1]
            target = cur if l < layers - 1 else wave_out.at[s]
            target[0] = real * w_real - imag * w_imag
            target[1] = real * w_imag + imag * w_real

        @pl.when(group < last)
        def _():
            wave_copy(s).start()

        @pl.when(group == last)
        def _():
            real, imag = two_sided(1, wave_out[s, 0], wave_out[s, 1])
            keep = live[s, 0:1, :] * (1.0 - amp[s] / jnp.sqrt(real * real + imag * imag + 1.0))
            cur[0] = real * keep
            cur[1] = -(imag * keep)
            real, imag = two_sided(1, cur[0], cur[1])
            chi_in[s, 0] = real
            chi_in[s, 1] = imag

    def adjoint(s):
        @pl.when(group < last)
        def _():
            chi_copy(s).wait_recv()

        for l in range(layers - 1, -1, -1):
            source = chi_in.at[s] if l == layers - 1 else cur
            c_real, c_imag = source[0], source[1]
            terms[s, l, 0] = psi[s, l, 0] * c_real - psi[s, l, 1] * c_imag
            terms[s, l, 1] = -(psi[s, l, 0] * c_imag + psi[s, l, 1] * c_real)
            term_copy(s, l).start()

            def back():
                w_real = win[s, l, 0] + nbr[s, l, 0]
                w_imag = win[s, l, 1] + nbr[s, l, 1]
                c_real, c_imag = source[0], source[1]
                return two_sided(0, w_real * c_real - w_imag * c_imag, w_real * c_imag + w_imag * c_real)

            if l > 0:
                real, imag = back()
                cur[0] = real
                cur[1] = imag
            else:

                @pl.when(group > 0)
                def _():
                    real, imag = back()
                    chi_out[s, 0] = real
                    chi_out[s, 1] = imag
                    chi_copy(s).start()

        for l in range(layers):
            add_terms(pos, terms, s, l, True)

    def task(k, carry):
        at_last = group * 2 >= groups
        is_forward = jnp.where(at_last, lax.rem(k, 2) == 0, k < slots)
        s = jnp.where(at_last, k // 2, lax.rem(k, slots))

        @pl.when(is_forward)
        def _():
            forward(s)

        @pl.when(jnp.logical_not(is_forward))
        def _():
            adjoint(s)

        return carry

    lax.fori_loop(0, 2 * slots, task, 0)

    for s in range(slots):
        for l in range(layers - 1, -1, -1):
            term_copy(s, l).wait_recv()
            add_terms(pos_in, terms_in, s, l, False)

    pos_copy.wait_send()
    for s in range(slots):
        for l in range(layers):
            if s == slots - 1:
                piece_copy(s, l).wait_send()
            term_copy(s, l).wait_send()

    @pl.when(group < last)
    def _():
        for s in range(slots):
            wave_copy(s).wait_send()

    @pl.when(group > 0)
    def _():
        for s in range(slots):
            chi_copy(s).wait_send()


def solution(mesh):
    tiles, groups = mesh.shape["scan"], mesh.shape["depth"]

    def body(probe, slices, positions, counts, amplitude):
        size = probe.shape[-1]
        slots = positions.shape[0]
        layers = slices.shape[0]
        places = jnp.broadcast_to(positions[:, :, None, None], (slots, 2, 8, size))
        live = (jnp.arange(slots, dtype=jnp.int32) < counts[0]).astype(jnp.float32)
        live = jnp.broadcast_to(live[:, None, None], (slots, 8, size))
        tables = [jnp.asarray(table) for table in make_tables(size)]
        planes = pltpu.VMEM((slots, layers, 2, size, size), jnp.float32)
        waves = pltpu.VMEM((slots, 2, size, size), jnp.float32)
        each = pltpu.SemaphoreType.DMA((slots, layers))
        some = pltpu.SemaphoreType.DMA((slots,))
        return pl.pallas_call(
            functools.partial(kernel, tiles, groups),
            out_shape=jax.ShapeDtypeStruct(slices.shape, jnp.float32),
            in_specs=[pl.BlockSpec(memory_space=pltpu.VMEM)] * 9,
            out_specs=pl.BlockSpec(memory_space=pltpu.VMEM),
            scratch_shapes=[
                planes, planes, planes, planes,
                waves, waves, waves, waves,
                planes, planes,
                pltpu.VMEM((slots, 2, 8, size), jnp.int32),
                pltpu.VMEM((2, size, size), jnp.float32),
                pltpu.SemaphoreType.DMA((2,)),
                each, each, some, some, some, some, each, each,
            ],
            compiler_params=pltpu.CompilerParams(
                collective_id=0, has_side_effects=True, vmem_limit_bytes=52 * 1024 * 1024
            ),
        )(probe, slices, places, amplitude, live, *tables)

    return jax.shard_map(
        body,
        mesh=mesh,
        in_specs=(
            P(),
            P("depth", None, ("groups", "scan"), None),
            P(("groups", "scan"), None),
            P(("groups", "scan")),
            P(("groups", "scan"), None, None),
        ),
        out_specs=P("depth", None, ("groups", "scan"), None),
        check_vma=False,
    )
```

```python
import functools
import math

import jax
import jax.numpy as jnp
import numpy as np
from jax import lax
from jax.experimental import pallas as pl
from jax.experimental.pallas import tpu as pltpu
from jax.sharding import PartitionSpec as P

chirp_rate = 0.25
CHUNK = 32


def make_tables(length):
    index = np.arange(length)
    angle = 2.0 * np.pi / length * (index[:, None] * index[None, :] % length)
    forward = (np.cos(angle) - 1j * np.sin(angle)) / math.sqrt(length)
    freq = np.where(index < length // 2, index, index - length).astype(np.float64)
    chirp = np.exp(-1j * np.pi * chirp_rate / length * freq**2)
    step = (np.conj(forward) * chirp[None, :]) @ forward
    left_hi, left_lo, right_hi, right_lo = [], [], [], []
    for table in (step, forward):
        real, imag = table.real, table.imag
        left = np.block([[real, -imag], [imag, real]]).astype(np.float32)
        right = np.block([[real, imag], [-imag, real]]).astype(np.float32)
        for whole, highs, lows in ((left, left_hi, left_lo), (right, right_hi, right_lo)):
            high = whole.astype(jnp.bfloat16)
            highs.append(high)
            lows.append((whole - high.astype(np.float32)).astype(jnp.bfloat16))
    return tuple(np.stack(parts) for parts in (left_hi, left_lo, right_hi, right_lo))


def dot(a, b):
    return jnp.dot(a, b, preferred_element_type=jnp.float32)


def split(x):
    high = x.astype(jnp.bfloat16)
    low = (x - high.astype(jnp.float32)).astype(jnp.bfloat16)
    return high, low


def kernel(
    tiles, groups,
    probe, slices, pos, amp, live, left_hi, left_lo, right_hi, right_lo,
    out,
    pieces, win, nbr, psi, wave_in, wave_out, chi_in, chi_out, terms, terms_in, pos_in, cur,
    pos_sem, piece_send, piece_recv, wave_send, wave_recv, chi_send, chi_recv, term_send, term_recv,
):
    slots, layers, _, size, _ = pieces.shape
    blocks = slices.shape[-1] // size
    tile = lax.axis_index("scan")
    group = lax.axis_index("depth")
    last = groups - 1
    next_tile = lax.rem(tile + 1, tiles)
    prev_tile = lax.rem(tile + tiles - 1, tiles)
    next_group = lax.rem(group + 1, groups)
    prev_group = lax.rem(group + groups - 1, groups)

    def remote(src, dst, send, recv, where):
        return pltpu.make_async_remote_copy(
            src_ref=src, dst_ref=dst, send_sem=send, recv_sem=recv,
            device_id=where, device_id_type=pl.DeviceIdType.MESH,
        )

    def piece_copy(s, l):
        return remote(pieces.at[s, l], nbr.at[s, l], piece_send.at[s, l], piece_recv.at[s, l], {"scan": prev_tile})

    def term_copy(s, l):
        return remote(terms.at[s, l], terms_in.at[s, l], term_send.at[s, l], term_recv.at[s, l], {"scan": next_tile})

    def wave_copy(s):
        return remote(wave_out.at[s], wave_in.at[s], wave_send.at[s], wave_recv.at[s], {"depth": next_group})

    def chi_copy(s):
        return remote(chi_out.at[s], chi_in.at[s], chi_send.at[s], chi_recv.at[s], {"depth": prev_group})

    barrier = pltpu.get_barrier_semaphore()
    for where in ({"scan": next_tile}, {"scan": prev_tile}, {"depth": next_group}, {"depth": prev_group}):
        pl.semaphore_signal(barrier, inc=1, device_id=where, device_id_type=pl.DeviceIdType.MESH)
    pl.semaphore_wait(barrier, 4)

    pos_copy = remote(pos, pos_in, pos_sem.at[0], pos_sem.at[1], {"scan": next_tile})
    pos_copy.start()

    def rows_of(chunk):
        return pl.ds(pl.multiple_of(chunk * CHUNK, CHUNK), CHUNK)

    def iotas(chunk):
        row = lax.broadcasted_iota(jnp.int32, (CHUNK, size), 0) + chunk * CHUNK
        column = lax.broadcasted_iota(jnp.int32, (CHUNK, size), 1)
        return row, column

    def inside(column, block, start):
        offset = column + block * size - start
        return (offset >= 0) & (offset < size)

    def cut(places, target, s, l, own):
        def one(chunk, carry):
            row, column = iotas(chunk)
            keep = row >= places[s, 0, 0:1, :]
            if not own:
                keep = jnp.logical_not(keep)
            start = places[s, 1, 0:1, :]
            for part in range(2):
                value = jnp.zeros((CHUNK, size), jnp.float32)
                for block in range(blocks):
                    value = jnp.where(
                        inside(column, block, start),
                        slices[l, part, rows_of(chunk), block * size : (block + 1) * size],
                        value,
                    )
                target[s, l, part, rows_of(chunk), :] = jnp.where(keep, value, 0.0)
            return carry

        lax.fori_loop(0, size // CHUNK, one, 0)

    def add_terms(places, source, s, l, own):
        def one(chunk, carry):
            row, column = iotas(chunk)
            keep = row >= places[s, 0, 0:1, :]
            if not own:
                keep = jnp.logical_not(keep)
            start = places[s, 1, 0:1, :]
            for part in range(2):
                value = jnp.where(keep, source[s, l, part, rows_of(chunk), :], 0.0)
                for block in range(blocks):
                    out[l, part, rows_of(chunk), block * size : (block + 1) * size] += jnp.where(
                        inside(column, block, start), value, 0.0
                    )
            return carry

        lax.fori_loop(0, size // CHUNK, one, 0)

    def two_sided(which, real, imag):
        high, low = split(jnp.concatenate([real, imag], axis=1))
        both = dot(jnp.concatenate([high, low], axis=0), right_hi[which])
        y = both[:size] + both[size:] + dot(high, right_lo[which])
        high, low = split(jnp.concatenate([y[:, :size], y[:, size:]], axis=0))
        left = jnp.concatenate([left_hi[which], left_lo[which]], axis=0)
        both = dot(left, high)
        z = both[: 2 * size] + both[2 * size :] + dot(left_hi[which], low)
        return z[:size], z[size:]

    pos_copy.wait_recv()

    for s in range(slots):
        for l in range(layers):
            cut(pos_in, pieces, s, l, False)
            if s == 0:
                piece_copy(s, l).start()

    out[...] = jnp.zeros_like(out)
    for s in range(slots):
        for l in range(layers):
            cut(pos, win, s, l, True)

    def roll_probe(s):
        row = lax.broadcasted_iota(jnp.int32, (size, size), 0)
        column = lax.broadcasted_iota(jnp.int32, (size, size), 1)
        down = row - column - pos[s, 0, 0:1, :]
        across = column - row - pos[s, 1, 0:1, :]
        rows_shift = jnp.zeros((size, size), jnp.float32)
        for turn in range(2):
            rows_shift = jnp.where(down == -turn * size, 1.0, rows_shift)
        columns_shift = jnp.zeros((size, size), jnp.float32)
        for turn in range(blocks + 1):
            columns_shift = jnp.where(across == -turn * size, 1.0, columns_shift)
        rows_shift = rows_shift.astype(jnp.bfloat16)
        columns_shift = columns_shift.astype(jnp.bfloat16)

        def three(x):
            first = x.astype(jnp.bfloat16)
            rest = x - first.astype(jnp.float32)
            second = rest.astype(jnp.bfloat16)
            third = (rest - second.astype(jnp.float32)).astype(jnp.bfloat16)
            return first, second, third

        for part in range(2):
            a, b, c = three(probe[part])
            x = dot(rows_shift, a) + dot(rows_shift, b) + dot(rows_shift, c)
            a, b, c = three(x)
            wave_in[s, part] = dot(a, columns_shift) + dot(b, columns_shift) + dot(c, columns_shift)

    def first_psi(s, carry):
        roll_probe(s)
        propagate(wave_in.at[s], s, 0)
        return carry

    def propagate(source, s, l):
        real, imag = two_sided(0, source[0], source[1])
        psi[s, l, 0] = real
        psi[s, l, 1] = imag

    @pl.when(group == 0)
    def _():
        lax.fori_loop(0, slots, first_psi, 0)

    for s in range(1, slots):
        for l in range(layers):
            piece_copy(s - 1, l).wait_send()
            piece_copy(s, l).start()

    def forward(s):
        @pl.when(group > 0)
        def _():
            wave_copy(s).wait_recv()
            propagate(wave_in.at[s], s, 0)

        for l in range(layers):
            if l > 0:
                propagate(cur, s, l)
            piece_copy(s, l).wait_recv()
            real, imag = psi[s, l, 0], psi[s, l, 1]
            w_real = win[s, l, 0] + nbr[s, l, 0]
            w_imag = win[s, l, 1] + nbr[s, l, 1]
            target = cur if l < layers - 1 else wave_out.at[s]
            target[0] = real * w_real - imag * w_imag
            target[1] = real * w_imag + imag * w_real

        @pl.when(group < last)
        def _():
            wave_copy(s).start()

        @pl.when(group == last)
        def _():
            real, imag = two_sided(1, wave_out[s, 0], wave_out[s, 1])
            keep = live[s, 0:1, :] * (1.0 - amp[s] / jnp.sqrt(real * real + imag * imag + 1.0))
            cur[0] = real * keep
            cur[1] = -(imag * keep)
            real, imag = two_sided(1, cur[0], cur[1])
            chi_in[s, 0] = real
            chi_in[s, 1] = imag

    def adjoint(s):
        @pl.when(group < last)
        def _():
            chi_copy(s).wait_recv()

        for l in range(layers - 1, -1, -1):
            source = chi_in.at[s] if l == layers - 1 else cur
            c_real, c_imag = source[0], source[1]
            terms[s, l, 0] = psi[s, l, 0] * c_real - psi[s, l, 1] * c_imag
            terms[s, l, 1] = -(psi[s, l, 0] * c_imag + psi[s, l, 1] * c_real)
            term_copy(s, l).start()

            def back():
                w_real = win[s, l, 0] + nbr[s, l, 0]
                w_imag = win[s, l, 1] + nbr[s, l, 1]
                c_real, c_imag = source[0], source[1]
                return two_sided(0, w_real * c_real - w_imag * c_imag, w_real * c_imag + w_imag * c_real)

            if l > 0:
                real, imag = back()
                cur[0] = real
                cur[1] = imag
            else:

                @pl.when(group > 0)
                def _():
                    real, imag = back()
                    chi_out[s, 0] = real
                    chi_out[s, 1] = imag
                    chi_copy(s).start()

    def task(k, carry):
        at_last = group * 2 >= groups
        is_forward = jnp.where(at_last, lax.rem(k, 2) == 0, k < slots)
        s = jnp.where(at_last, k // 2, lax.rem(k, slots))

        @pl.when(is_forward)
        def _():
            forward(s)

        @pl.when(jnp.logical_not(is_forward))
        def _():
            adjoint(s)

        return carry

    lax.fori_loop(0, 2 * slots, task, 0)

    for s in range(slots):
        for l in range(layers - 1, -1, -1):
            add_terms(pos, terms, s, l, True)
    for s in range(slots):
        for l in range(layers - 1, -1, -1):
            term_copy(s, l).wait_recv()
            add_terms(pos_in, terms_in, s, l, False)

    pos_copy.wait_send()
    for s in range(slots):
        for l in range(layers):
            if s == slots - 1:
                piece_copy(s, l).wait_send()
            term_copy(s, l).wait_send()

    @pl.when(group < last)
    def _():
        for s in range(slots):
            wave_copy(s).wait_send()

    @pl.when(group > 0)
    def _():
        for s in range(slots):
            chi_copy(s).wait_send()


def solution(mesh):
    tiles, groups = mesh.shape["scan"], mesh.shape["depth"]

    def body(probe, slices, positions, counts, amplitude):
        size = probe.shape[-1]
        slots = positions.shape[0]
        layers = slices.shape[0]
        places = jnp.broadcast_to(positions[:, :, None, None], (slots, 2, 8, size))
        live = (jnp.arange(slots, dtype=jnp.int32) < counts[0]).astype(jnp.float32)
        live = jnp.broadcast_to(live[:, None, None], (slots, 8, size))
        tables = [jnp.asarray(table) for table in make_tables(size)]
        planes = pltpu.VMEM((slots, layers, 2, size, size), jnp.float32)
        waves = pltpu.VMEM((slots, 2, size, size), jnp.float32)
        each = pltpu.SemaphoreType.DMA((slots, layers))
        some = pltpu.SemaphoreType.DMA((slots,))
        return pl.pallas_call(
            functools.partial(kernel, tiles, groups),
            out_shape=jax.ShapeDtypeStruct(slices.shape, jnp.float32),
            in_specs=[pl.BlockSpec(memory_space=pltpu.VMEM)] * 9,
            out_specs=pl.BlockSpec(memory_space=pltpu.VMEM),
            scratch_shapes=[
                planes, planes, planes, planes,
                waves, waves, waves, waves,
                planes, planes,
                pltpu.VMEM((slots, 2, 8, size), jnp.int32),
                pltpu.VMEM((2, size, size), jnp.float32),
                pltpu.SemaphoreType.DMA((2,)),
                each, each, some, some, some, some, each, each,
            ],
            compiler_params=pltpu.CompilerParams(
                collective_id=0, has_side_effects=True, vmem_limit_bytes=52 * 1024 * 1024
            ),
        )(probe, slices, places, amplitude, live, *tables)

    return jax.shard_map(
        body,
        mesh=mesh,
        in_specs=(
            P(),
            P("depth", None, ("groups", "scan"), None),
            P(("groups", "scan"), None),
            P(("groups", "scan")),
            P(("groups", "scan"), None, None),
        ),
        out_specs=P("depth", None, ("groups", "scan"), None),
        check_vma=False,
    )
```

```python
import functools
import math

import jax
import jax.numpy as jnp
import numpy as np
from jax import lax
from jax.experimental import pallas as pl
from jax.experimental.pallas import tpu as pltpu
from jax.sharding import PartitionSpec as P

chirp_rate = 0.25
CHUNK = 32


def make_tables(length):
    index = np.arange(length)
    angle = 2.0 * np.pi / length * (index[:, None] * index[None, :] % length)
    forward = (np.cos(angle) - 1j * np.sin(angle)) / math.sqrt(length)
    freq = np.where(index < length // 2, index, index - length).astype(np.float64)
    chirp = np.exp(-1j * np.pi * chirp_rate / length * freq**2)
    step = (np.conj(forward) * chirp[None, :]) @ forward
    left_hi, left_lo, right_hi, right_lo = [], [], [], []
    for table in (step, forward):
        real, imag = table.real, table.imag
        left = np.block([[real, -imag], [imag, real]]).astype(np.float32)
        right = np.block([[real, imag], [-imag, real]]).astype(np.float32)
        for whole, highs, lows in ((left, left_hi, left_lo), (right, right_hi, right_lo)):
            high = whole.astype(jnp.bfloat16)
            highs.append(high)
            lows.append((whole - high.astype(np.float32)).astype(jnp.bfloat16))
    return tuple(np.stack(parts) for parts in (left_hi, left_lo, right_hi, right_lo))


def dot(a, b):
    return jnp.dot(a, b, preferred_element_type=jnp.float32)


def split(x):
    high = x.astype(jnp.bfloat16)
    low = (x - high.astype(jnp.float32)).astype(jnp.bfloat16)
    return high, low


def kernel(
    tiles, groups,
    probe, slices, pos, amp, live, left_hi, left_lo, right_hi, right_lo,
    out,
    pieces, win, nbr, psi, wave_in, wave_out, chi_in, chi_out, terms, terms_in, pos_in, cur,
    pos_sem, piece_send, piece_recv, wave_send, wave_recv, chi_send, chi_recv, term_send, term_recv,
):
    slots, layers, _, size, _ = pieces.shape
    blocks = slices.shape[-1] // size
    tile = lax.axis_index("scan")
    group = lax.axis_index("depth")
    last = groups - 1
    next_tile = lax.rem(tile + 1, tiles)
    prev_tile = lax.rem(tile + tiles - 1, tiles)
    next_group = lax.rem(group + 1, groups)
    prev_group = lax.rem(group + groups - 1, groups)

    def remote(src, dst, send, recv, where):
        return pltpu.make_async_remote_copy(
            src_ref=src, dst_ref=dst, send_sem=send, recv_sem=recv,
            device_id=where, device_id_type=pl.DeviceIdType.MESH,
        )

    def piece_copy(s, l):
        return remote(pieces.at[s, l], nbr.at[s, l], piece_send.at[s, l], piece_recv.at[s, l], {"scan": prev_tile})

    def term_copy(s, l):
        return remote(terms.at[s, l], terms_in.at[s, l], term_send.at[s, l], term_recv.at[s, l], {"scan": next_tile})

    def wave_copy(s):
        return remote(wave_out.at[s], wave_in.at[s], wave_send.at[s], wave_recv.at[s], {"depth": next_group})

    def chi_copy(s):
        return remote(chi_out.at[s], chi_in.at[s], chi_send.at[s], chi_recv.at[s], {"depth": prev_group})

    barrier = pltpu.get_barrier_semaphore()
    for where in ({"scan": next_tile}, {"scan": prev_tile}, {"depth": next_group}, {"depth": prev_group}):
        pl.semaphore_signal(barrier, inc=1, device_id=where, device_id_type=pl.DeviceIdType.MESH)
    pl.semaphore_wait(barrier, 4)

    pos_copy = remote(pos, pos_in, pos_sem.at[0], pos_sem.at[1], {"scan": next_tile})
    pos_copy.start()

    def rows_of(chunk):
        return pl.ds(pl.multiple_of(chunk * CHUNK, CHUNK), CHUNK)

    def iotas(chunk):
        row = lax.broadcasted_iota(jnp.int32, (CHUNK, size), 0) + chunk * CHUNK
        column = lax.broadcasted_iota(jnp.int32, (CHUNK, size), 1)
        return row, column

    def inside(column, block, start):
        offset = column + block * size - start
        return (offset >= 0) & (offset < size)

    def cut(places, target, s, l, own):
        def one(chunk, carry):
            row, column = iotas(chunk)
            keep = row >= places[s, 0, 0:1, :]
            if not own:
                keep = jnp.logical_not(keep)
            start = places[s, 1, 0:1, :]
            for part in range(2):
                value = jnp.zeros((CHUNK, size), jnp.float32)
                for block in range(blocks):
                    value = jnp.where(
                        inside(column, block, start),
                        slices[l, part, rows_of(chunk), block * size : (block + 1) * size],
                        value,
                    )
                target[s, l, part, rows_of(chunk), :] = jnp.where(keep, value, 0.0)
            return carry

        lax.fori_loop(0, size // CHUNK, one, 0)

    def add_terms(places, source, s, l, own):
        def one(chunk, carry):
            row, column = iotas(chunk)
            keep = row >= places[s, 0, 0:1, :]
            if not own:
                keep = jnp.logical_not(keep)
            start = places[s, 1, 0:1, :]
            for part in range(2):
                value = jnp.where(keep, source[s, l, part, rows_of(chunk), :], 0.0)
                for block in range(blocks):
                    out[l, part, rows_of(chunk), block * size : (block + 1) * size] += jnp.where(
                        inside(column, block, start), value, 0.0
                    )
            return carry

        lax.fori_loop(0, size // CHUNK, one, 0)

    def two_sided(which, real, imag):
        high, low = split(jnp.concatenate([real, imag], axis=1))
        both = dot(jnp.concatenate([high, low], axis=0), right_hi[which])
        y = both[:size] + both[size:] + dot(high, right_lo[which])
        high, low = split(jnp.concatenate([y[:, :size], y[:, size:]], axis=0))
        left = jnp.concatenate([left_hi[which], left_lo[which]], axis=0)
        both = dot(left, high)
        z = both[: 2 * size] + both[2 * size :] + dot(left_hi[which], low)
        return z[:size], z[size:]

    pos_copy.wait_recv()

    for s in range(slots):
        for l in range(layers):
            cut(pos_in, pieces, s, l, False)
            if s == 0:
                piece_copy(s, l).start()

    out[...] = jnp.zeros_like(out)
    for s in range(slots):
        for l in range(layers):
            cut(pos, win, s, l, True)

    def roll_probe(s):
        row = lax.broadcasted_iota(jnp.int32, (size, size), 0)
        column = lax.broadcasted_iota(jnp.int32, (size, size), 1)
        down = row - column - pos[s, 0, 0:1, :]
        across = column - row - pos[s, 1, 0:1, :]
        rows_shift = jnp.zeros((size, size), jnp.float32)
        for turn in range(2):
            rows_shift = jnp.where(down == -turn * size, 1.0, rows_shift)
        columns_shift = jnp.zeros((size, size), jnp.float32)
        for turn in range(blocks + 1):
            columns_shift = jnp.where(across == -turn * size, 1.0, columns_shift)
        rows_shift = rows_shift.astype(jnp.bfloat16)
        columns_shift = columns_shift.astype(jnp.bfloat16)

        def three(x):
            first = x.astype(jnp.bfloat16)
            rest = x - first.astype(jnp.float32)
            second = rest.astype(jnp.bfloat16)
            third = (rest - second.astype(jnp.float32)).astype(jnp.bfloat16)
            return first, second, third

        for part in range(2):
            a, b, c = three(probe[part])
            x = dot(rows_shift, a) + dot(rows_shift, b) + dot(rows_shift, c)
            a, b, c = three(x)
            wave_in[s, part] = dot(a, columns_shift) + dot(b, columns_shift) + dot(c, columns_shift)

    def first_psi(s, carry):
        roll_probe(s)
        propagate(wave_in.at[s], s, 0)
        return carry

    def propagate(source, s, l):
        real, imag = two_sided(0, source[0], source[1])
        psi[s, l, 0] = real
        psi[s, l, 1] = imag

    @pl.when(group == 0)
    def _():
        lax.fori_loop(0, slots, first_psi, 0)

    for s in range(1, slots):
        for l in range(layers):
            piece_copy(s - 1, l).wait_send()
            piece_copy(s, l).start()

    def forward(s):
        @pl.when(group > 0)
        def _():
            wave_copy(s).wait_recv()
            propagate(wave_in.at[s], s, 0)

        for l in range(layers):
            if l > 0:
                propagate(cur, s, l)
            piece_copy(s, l).wait_recv()
            real, imag = psi[s, l, 0], psi[s, l, 1]
            w_real = win[s, l, 0] + nbr[s, l, 0]
            w_imag = win[s, l, 1] + nbr[s, l, 1]
            target = cur if l < layers - 1 else wave_out.at[s]
            target[0] = real * w_real - imag * w_imag
            target[1] = real * w_imag + imag * w_real

        @pl.when(group < last)
        def _():
            wave_copy(s).start()

        @pl.when(group == last)
        def _():
            real, imag = two_sided(1, wave_out[s, 0], wave_out[s, 1])
            keep = live[s, 0:1, :] * (1.0 - amp[s] / jnp.sqrt(real * real + imag * imag + 1.0))
            cur[0] = real * keep
            cur[1] = -(imag * keep)
            real, imag = two_sided(1, cur[0], cur[1])
            chi_in[s, 0] = real
            chi_in[s, 1] = imag

    def adjoint(s):
        @pl.when(group < last)
        def _():
            chi_copy(s).wait_recv()

        for l in range(layers - 1, -1, -1):
            source = chi_in.at[s] if l == layers - 1 else cur
            c_real, c_imag = source[0], source[1]
            terms[s, l, 0] = psi[s, l, 0] * c_real - psi[s, l, 1] * c_imag
            terms[s, l, 1] = -(psi[s, l, 0] * c_imag + psi[s, l, 1] * c_real)
            term_copy(s, l).start()

            def back():
                w_real = win[s, l, 0] + nbr[s, l, 0]
                w_imag = win[s, l, 1] + nbr[s, l, 1]
                c_real, c_imag = source[0], source[1]
                return two_sided(0, w_real * c_real - w_imag * c_imag, w_real * c_imag + w_imag * c_real)

            if l > 0:
                real, imag = back()
                cur[0] = real
                cur[1] = imag
            else:

                @pl.when(group > 0)
                def _():
                    real, imag = back()
                    chi_out[s, 0] = real
                    chi_out[s, 1] = imag
                    chi_copy(s).start()

        for l in range(layers):
            add_terms(pos, terms, s, l, True)

    def task(k, carry):
        at_last = group * 2 >= groups
        is_forward = jnp.where(at_last, lax.rem(k, 2) == 0, k < slots)
        s = jnp.where(at_last, k // 2, lax.rem(k, slots))

        @pl.when(is_forward)
        def _():
            forward(s)

        @pl.when(jnp.logical_not(is_forward))
        def _():
            adjoint(s)

        return carry

    lax.fori_loop(0, 2 * slots, task, 0)

    for s in range(slots):
        for l in range(layers - 1, -1, -1):
            term_copy(s, l).wait_recv()
            add_terms(pos_in, terms_in, s, l, False)

    pos_copy.wait_send()
    for s in range(slots):
        for l in range(layers):
            if s == slots - 1:
                piece_copy(s, l).wait_send()
            term_copy(s, l).wait_send()

    @pl.when(group < last)
    def _():
        for s in range(slots):
            wave_copy(s).wait_send()

    @pl.when(group > 0)
    def _():
        for s in range(slots):
            chi_copy(s).wait_send()


def solution(mesh):
    tiles, groups = mesh.shape["scan"], mesh.shape["depth"]

    def body(probe, slices, positions, counts, amplitude):
        size = probe.shape[-1]
        slots = positions.shape[0]
        layers = slices.shape[0]
        places = jnp.broadcast_to(positions[:, :, None, None], (slots, 2, 8, size))
        live = (jnp.arange(slots, dtype=jnp.int32) < counts[0]).astype(jnp.float32)
        live = jnp.broadcast_to(live[:, None, None], (slots, 8, size))
        tables = [jnp.asarray(table) for table in make_tables(size)]
        planes = pltpu.VMEM((slots, layers, 2, size, size), jnp.float32)
        waves = pltpu.VMEM((slots, 2, size, size), jnp.float32)
        each = pltpu.SemaphoreType.DMA((slots, layers))
        some = pltpu.SemaphoreType.DMA((slots,))
        return pl.pallas_call(
            functools.partial(kernel, tiles, groups),
            out_shape=jax.ShapeDtypeStruct(slices.shape, jnp.float32),
            in_specs=[pl.BlockSpec(memory_space=pltpu.VMEM)] * 9,
            out_specs=pl.BlockSpec(memory_space=pltpu.VMEM),
            scratch_shapes=[
                planes, planes, planes, planes,
                waves, waves, waves, waves,
                planes, planes,
                pltpu.VMEM((slots, 2, 8, size), jnp.int32),
                pltpu.VMEM((2, size, size), jnp.float32),
                pltpu.SemaphoreType.DMA((2,)),
                each, each, some, some, some, some, each, each,
            ],
            compiler_params=pltpu.CompilerParams(
                collective_id=0, has_side_effects=True, vmem_limit_bytes=52 * 1024 * 1024
            ),
        )(probe, slices, places, amplitude, live, *tables)

    return jax.shard_map(
        body,
        mesh=mesh,
        in_specs=(
            P(),
            P("depth", None, ("groups", "scan"), None),
            P(("groups", "scan"), None),
            P(("groups", "scan")),
            P(("groups", "scan"), None, None),
        ),
        out_specs=P("depth", None, ("groups", "scan"), None),
        check_vma=False,
    )
```
